32 devices in a mesh: prow: 4 (over y, x), pcol: 8 (over z, core).
Axes of the slice: x: 2, y: 2, z: 4, core: 2. Of those that a mesh axis runs over, the one named last changes fastest.
Arguments:
- inverse_panel: float32 [1024, 4, 8, 32], P('prow', None, 'pcol'), may hold values from -6 to 6
- lower_blocks: float32 [4, 8, 32, 2048], P('prow', None, None, 'pcol'), may hold values from -0.25 to 0.25
- diag_inverse: float32 [2048, 128], P('pcol'), may hold values from -6 to 6
- pattern: int32 [8, 16], replicated, may hold values 0 or 1
- widths: int32 [16], replicated, may hold values from 1 to 128, 1536 in all
Outputs:
- selected_rows: float32 [2048, 1024], P('pcol', 'prow')
- diag_block: float32 [2048, 128], P('pcol')
The draws below stay inside these ranges and needn't reach their ends.
All inputs are finite; a program needn't handle non-finite values.
Results may differ from the reference program's by a relative error of at most 0.00007.
Values sent between devices are 32-bit elements; how exact they have to be, the bound alone decides.
No kernel may reach another device: no remote copies, remote signals or barrier semaphores. Data moves between devices by JAX's collectives and lax.ppermute only.
A program may use at most 128 MiB of HBM per device.

```python
import math
import jax
import jax.numpy as jnp
import numpy as np
from jax import lax

BLK = 128
TR = 32
N = 1024
S = 16
W = 2048
NB = 8
N_PROW = 4
N_PCOL = 8


def touch_ends(entries, key, smallest, top_value):
    extent = entries.shape
    spot = [jax.random.randint(jax.random.fold_in(key, axis), (), 0, extent[axis]) for axis in range(len(extent))]
    entries = entries.at[tuple(spot)].set(smallest)
    longest = extent.index(max(extent))
    spot[longest] = (spot[longest] + 1) % extent[longest]
    return entries.at[tuple(spot)].set(top_value)


def block_levels(own_key, shape, split, low, top_value):
    gain = 1.0
    for position, shards_of in split:
        draws = jax.random.uniform(jax.random.fold_in(jax.random.fold_in(own_key, 6), position), (shards_of,), jnp.float32, low / len(split), top_value / len(split))
        gain = gain * jnp.repeat(jnp.exp(draws), shape[position] // shards_of).reshape((-1,) + (1,) * (len(shape) - 1 - position))
    return gain


def split_up(number_of, total, limit, skew):
    loads = [(1 << 20) // math.isqrt(standing ** skew) + 1 for standing in range(2, number_of + 1)]
    surplus, given = total - limit - (number_of - 1), [1] * (number_of - 1)
    while surplus > 0:
        free = [i for i in range(number_of - 1) if given[i] < limit]
        pool, remaining = sum([loads[i] for i in free]), surplus
        for i in free:
            addition = min(limit - given[i], max(1, remaining * loads[i] // pool), surplus)
            given[i] = given[i] + addition
            surplus = surplus - addition
    return np.array([limit] + given)


def ragged(key, count, total, bound, skew):
    if count == 2:
        one = jax.random.randint(key, (), max(1, total - bound), min(bound, total - 1) + 1)
        return jnp.stack([one, total - one])
    lengths = jnp.asarray(split_up(count, total, bound, skew), jnp.int32)
    twos = (count - 1) // 2
    giver, taker = lengths[1:1 + 2 * twos:2], lengths[2:2 + 2 * twos:2]
    slack = jnp.minimum(giver - 1, bound - taker)
    passed = jax.random.randint(jax.random.fold_in(key, 1), (twos,), 0, 1 << 20) % (slack + 1)
    lengths = lengths.at[1:1 + 2 * twos:2].set(giver - passed).at[2:2 + 2 * twos:2].set(taker + passed)
    return lengths[jax.random.permutation(jax.random.fold_in(key, 2), count)]


def normal_values(key, dims, scale, limit, split=(), kind=jnp.bfloat16):
    drawn = jax.random.normal(key, dims, jnp.float32) * scale
    if len(split) > 0:
        drawn = block_levels(key, dims, split, -0.22, 0.18) * drawn
    return jnp.clip(drawn, min=-limit, max=limit).astype(kind)


def setup_inputs(seed: int = 0) -> dict:
    key_of = jax.random.split(jax.random.key(seed), 6)
    return {
        "inverse_panel": normal_values(key_of[0], (N, N_PROW, N_PCOL, TR), 1.0, 6.0, ((0, 4), (2, 8)), jnp.float32),
        "lower_blocks": normal_values(key_of[1], (N_PROW, N_PCOL, TR, W), (N // 2) ** -0.5, 0.25, ((0, 4), (3, 8)), jnp.float32),
        "diag_inverse": normal_values(key_of[2], (W, BLK), 1.0, 6.0, ((0, 8),), jnp.float32),
        "pattern": touch_ends((jax.random.randint(key_of[3], (NB, S), 0, 2) < 1).astype(jnp.int32), jax.random.fold_in(key_of[3], 1), 0, 1),
        "widths": ragged(key_of[4], S, 96 * S, BLK, 2).astype(jnp.int32),
    }


def reference(inverse_panel, lower_blocks, diag_inverse, pattern, widths):
    ainv = inverse_panel.reshape(N, N)
    lower = lower_blocks.reshape(N, W)
    block_ids = jnp.arange(N, dtype=jnp.int32) // BLK
    row_pattern = pattern[block_ids].astype(jnp.float32)
    row_expand = jnp.repeat(row_pattern, BLK, axis=1)
    alive = (jnp.arange(BLK, dtype=jnp.int32)[None, :] < widths[:, None]).astype(jnp.float32)
    mask = row_expand * alive.reshape(W)[None, :]
    masked = lower * mask
    product = jnp.dot(ainv, masked, precision=lax.Precision.HIGHEST, preferred_element_type=jnp.float32)
    selected = (-product * mask).T
    sel_blocks = selected.reshape(S, BLK, N)
    low_blocks = masked.reshape(N, S, BLK)
    crossed = jnp.einsum("skn,nsj->skj", sel_blocks, low_blocks, precision=lax.Precision.HIGHEST)
    both_alive = alive[:, :, None] * alive[:, None, :]
    diag_out = (diag_inverse.reshape(S, BLK, BLK) - crossed) * both_alive
    return selected, diag_out.reshape(W, BLK)
```

```python
import functools
import jax
import jax.numpy as jnp
from jax import lax
from jax.experimental import pallas as pl
from jax.experimental.pallas import tpu as pltpu
from jax.sharding import PartitionSpec as P

ROW_STEP = 256
DEPTH_STEP = 1024


def offset_of(order, block):
    total = 0
    for place, bit in enumerate(order):
        if block >> place & 1:
            total ^= bit
    return total


def split(values):
    high = values.astype(jnp.bfloat16)
    return high, (values - high.astype(jnp.float32)).astype(jnp.bfloat16)


def dot3(a, b, dims):
    (a_high, a_low), (b_high, b_low) = a, b
    dot = functools.partial(
        lax.dot_general, dimension_numbers=(dims, ((), ())), preferred_element_type=jnp.float32
    )
    return dot(a_high, b_high) + (dot(a_high, b_low) + dot(a_low, b_high))


def kernel(shape, orders, *refs):
    row_count, col_count, run, block_len, sup_here = shape
    row_orders, col_orders = orders
    panel_refs, refs = refs[:col_count], refs[col_count:]
    lower_refs, refs = refs[:row_count], refs[row_count:]
    pattern_ref, widths_ref, sel_ref, cross_ref, lh, ll, ah, al = refs
    step = pl.program_id(0)
    row = lax.axis_index("prow")
    col = lax.axis_index("pcol")
    core = lax.rem(col, 2)
    rows_here = col_count * run
    sup = col * sup_here
    lanes = lax.broadcasted_iota(jnp.int32, (block_len, block_len), 1)
    subs = lax.broadcasted_iota(jnp.int32, (block_len, block_len), 0)

    @pl.when(step == 0)
    def _():
        for block, ref in enumerate(lower_refs):
            source = row ^ jnp.where(
                core == 0, offset_of(row_orders[0], block), offset_of(row_orders[1], block)
            )

            @pl.loop(0, rows_here // block_len)
            def _(part):
                base = source * rows_here + part * block_len
                base = pl.multiple_of(base, block_len)
                here = pl.multiple_of(part * block_len, block_len)
                for s in range(sup_here):
                    cols = slice(s * block_len, (s + 1) * block_len)
                    kept = jnp.where(
                        pattern_ref[base // block_len, sup + s] != 0, widths_ref[sup + s], 0
                    )
                    values = jnp.where(lanes < kept, ref[pl.ds(here, block_len), cols], 0.0)
                    high, low = split(values)
                    lh[pl.ds(base, block_len), cols] = high
                    ll[pl.ds(base, block_len), cols] = low

    half = col_count // 2
    for number, ref in enumerate(panel_refs):
        block, other = number % half, number // half
        first, second = (offset_of(order, block) for order in col_orders)
        if other:
            source = col ^ 1 ^ jnp.where(core == 0, second, first)
        else:
            source = col ^ jnp.where(core == 0, first, second)
        for i in range(row_count):
            high, low = split(ref[i * run : (i + 1) * run, :])
            base = pl.multiple_of(i * rows_here + source * run, run)
            ah[pl.ds(base, run), :] = high
            al[pl.ds(base, run), :] = low

    width = sup_here * block_len
    total = None
    depth = row_count * rows_here
    chunk = min(depth, DEPTH_STEP)

    def product(base):
        here = pl.ds(base, chunk)
        return dot3((lh[here, :], ll[here, :]), (ah[here, :], al[here, :]), ((0,), (0,)))

    if depth == chunk:
        total = product(0)
    else:
        total = lax.fori_loop(
            0,
            depth // chunk,
            lambda c, acc: acc + product(pl.multiple_of(c * chunk, chunk)),
            jnp.zeros((width, ROW_STEP), jnp.float32),
        )
    mine = row * rows_here + step * ROW_STEP
    for s in range(sup_here):
        cols = slice(s * block_len, (s + 1) * block_len)
        crossed = None
        for part in range(ROW_STEP // block_len):
            piece = total[cols, part * block_len : (part + 1) * block_len]
            base = pl.multiple_of(mine + part * block_len, block_len)
            kept = jnp.where(pattern_ref[base // block_len, sup + s] != 0, widths_ref[sup + s], 0)
            chosen = jnp.where(subs < kept, -piece, 0.0)
            sel_ref[cols, part * block_len : (part + 1) * block_len] = chosen
            here = pl.ds(base, block_len)
            term = dot3(split(chosen), (lh[here, cols], ll[here, cols]), ((1,), (0,)))
            crossed = term if crossed is None else crossed + term

        @pl.when(step == 0)
        def _():
            cross_ref[cols, :] = crossed

        @pl.when(step != 0)
        def _():
            cross_ref[cols, :] += crossed


def per_device(mesh_sizes, inverse_panel, lower_blocks, diag_inverse, pattern, widths):
    row_count, col_count = mesh_sizes
    rows_here, _, _, run = inverse_panel.shape
    width = lower_blocks.shape[3]
    block_len = diag_inverse.shape[1]
    sup_here = width // block_len
    col_index = lax.axis_index("pcol")

    row_bits = [1 << b for b in range(row_count.bit_length() - 1)]
    col_bits = [1 << b for b in range(1, col_count.bit_length() - 1)][::-1]
    row_orders = (row_bits, row_bits[::-1])
    col_orders = (col_bits, col_bits[::-1])

    def send(values, row_steps, col_steps):
        pairs = []
        for r in range(row_count):
            for c in range(col_count):
                target = (r ^ row_steps[c % 2]) * col_count + (c ^ col_steps[c % 2])
                pairs.append((r * col_count + c, target))
        return lax.ppermute(values, ("prow", "pcol"), pairs)

    def along_rows(values, place):
        return send(values, [order[place] for order in row_orders], (0, 0))

    def along_cols(values, place):
        return send(values, (0, 0), [order[place] for order in col_orders])

    def gathered(own, places, move):
        held = [own]
        for place in range(places):
            held = held + [move(values, place) for values in held]
        return held

    panel = jnp.transpose(inverse_panel, (1, 2, 3, 0)).reshape(row_count * run, rows_here)
    lower = lower_blocks.reshape(rows_here, width)
    lowers = gathered(lower, len(row_bits), along_rows)
    panels = gathered(panel, len(col_bits), along_cols)
    panels = panels + [send(values, (0, 0), (1, 1)) for values in panels]

    depth = row_count * rows_here
    smem = pl.BlockSpec(memory_space=pltpu.SMEM)
    flops = 6 * depth * width * rows_here
    selected, crossed = pl.pallas_call(
        functools.partial(
            kernel,
            (row_count, col_count, run, block_len, sup_here),
            (row_orders, col_orders),
        ),
        grid=(rows_here // ROW_STEP,),
        in_specs=[pl.BlockSpec((row_count * run, ROW_STEP), lambda i: (0, i))] * col_count
        + [pl.BlockSpec((rows_here, width), lambda i: (0, 0), pipeline_mode=pl.Buffered(1))]
        * row_count
        + [smem, smem],
        out_specs=[
            pl.BlockSpec((width, ROW_STEP), lambda i: (0, i)),
            pl.BlockSpec((width, block_len), lambda i: (0, 0)),
        ],
        out_shape=[
            jax.ShapeDtypeStruct((width, rows_here), jnp.float32),
            jax.ShapeDtypeStruct((width, block_len), jnp.float32),
        ],
        scratch_shapes=[pltpu.VMEM((depth, width), jnp.bfloat16)] * 2
        + [pltpu.VMEM((depth, ROW_STEP), jnp.bfloat16)] * 2,
        compiler_params=pltpu.CompilerParams(vmem_limit_bytes=56 << 20),
        cost_estimate=pl.CostEstimate(
            flops=flops, bytes_accessed=4 * depth * (width + rows_here), transcendentals=0
        ),
    )(*panels, *lowers, pattern, widths)

    for place in range(len(row_bits)):
        crossed = crossed + along_rows(crossed, place)
    widths_local = lax.dynamic_slice_in_dim(widths, col_index * sup_here, sup_here, 0)
    alive = jnp.arange(block_len, dtype=jnp.int32)[None, :] < widths_local[:, None]
    both_alive = alive[:, :, None] & alive[:, None, :]
    shape = (sup_here, block_len, block_len)
    difference = diag_inverse.reshape(shape) - crossed.reshape(shape)
    diag_out = jnp.where(both_alive, difference, 0.0)
    return selected, diag_out.reshape(width, block_len)


def solution(mesh):
    placed = (
        P("prow", None, "pcol", None),
        P("prow", None, None, "pcol"),
        P("pcol", None),
        P(),
        P(),
    )
    return jax.shard_map(
        functools.partial(per_device, (mesh.shape["prow"], mesh.shape["pcol"])),
        mesh=mesh,
        in_specs=placed,
        out_specs=(P("pcol", "prow"), P("pcol", None)),
        check_vma=False,
    )
```

```python
import functools
import jax
import jax.numpy as jnp
from jax import lax
from jax.experimental import pallas as pl
from jax.experimental.pallas import tpu as pltpu
from jax.sharding import PartitionSpec as P

ROW_STEP = 256


def offset_of(order, block):
    total = 0
    for place, bit in enumerate(order):
        if block >> place & 1:
            total ^= bit
    return total


def split(values):
    high = values.astype(jnp.bfloat16)
    return high, (values - high.astype(jnp.float32)).astype(jnp.bfloat16)


def dot3(a, b, dims):
    (a_high, a_low), (b_high, b_low) = a, b
    dot = functools.partial(
        lax.dot_general, dimension_numbers=(dims, ((), ())), preferred_element_type=jnp.float32
    )
    return dot(a_high, b_high) + (dot(a_high, b_low) + dot(a_low, b_high))


def kept_columns(pattern_ref, widths_ref, row_block, sup):
    return jnp.where(pattern_ref[row_block, sup] != 0, widths_ref[sup], 0)


def rows_of_pair(ref, source, run, rows_here, row_count):
    pieces = []
    for column in (source, source ^ 1):
        for i in range(row_count):
            base = pl.multiple_of(i * rows_here + column * run, run)
            pieces.append(ref[pl.ds(base, run), :])
    return jnp.concatenate(pieces, axis=0)


def pair_product(lowers, own_ref, other_ref):
    panel = split(jnp.concatenate([own_ref[...], other_ref[...]], axis=0))
    return dot3(lowers, panel, ((0,), (0,)))


def early_kernel(shape, row_orders, col_offsets, *refs):
    row_count, col_count, run, block_len, sup_here = shape
    half = col_count // 2
    panel_refs, refs = refs[: 2 * (half - 1)], refs[2 * (half - 1) :]
    lower_refs, refs = refs[:row_count], refs[row_count:]
    pattern_ref, widths_ref, total_ref, lx_high, lx_low, lm_high, lm_low, lh, ll = refs
    row = lax.axis_index("prow")
    col = lax.axis_index("pcol")
    core = lax.rem(col, 2)
    rows_here = col_count * run
    sup = col * sup_here
    lanes = lax.broadcasted_iota(jnp.int32, (block_len, block_len), 1)

    @pl.when(pl.program_id(0) == 0)
    def _():
        for block, ref in enumerate(lower_refs):
            first, second = (offset_of(order, block) for order in row_orders)
            source = row ^ jnp.where(core == 0, first, second)
            for part in range(rows_here // block_len):
                base = pl.multiple_of(source * rows_here + part * block_len, block_len)
                here = slice(part * block_len, (part + 1) * block_len)
                for s in range(sup_here):
                    cols = slice(s * block_len, (s + 1) * block_len)
                    kept = kept_columns(pattern_ref, widths_ref, base // block_len, sup + s)
                    high, low = split(jnp.where(lanes < kept, ref[here, cols], 0.0))
                    lh[pl.ds(base, block_len), cols] = high
                    ll[pl.ds(base, block_len), cols] = low
                    if block == 0:
                        lm_high[here, cols] = high
                        lm_low[here, cols] = low
        late = col ^ col_offsets[-1]
        lx_high[...] = rows_of_pair(lh, late, run, rows_here, row_count)
        lx_low[...] = rows_of_pair(ll, late, run, rows_here, row_count)

    total = None
    for block in range(half - 1):
        source = col ^ col_offsets[block]
        lowers = tuple(rows_of_pair(ref, source, run, rows_here, row_count) for ref in (lh, ll))
        part = pair_product(lowers, panel_refs[2 * block], panel_refs[2 * block + 1])
        total = part if total is None else total + part
    total_ref[...] = total


def late_kernel(shape, *refs):
    row_count, col_count, run, block_len, sup_here = shape
    total_ref, lx_high, lx_low, lm_high, lm_low, own_ref, other_ref, *refs = refs
    pattern_ref, widths_ref, sel_ref, cross_ref = refs
    step = pl.program_id(0)
    row = lax.axis_index("prow")
    rows_here = col_count * run
    sup = lax.axis_index("pcol") * sup_here
    subs = lax.broadcasted_iota(jnp.int32, (block_len, block_len), 0)
    total = total_ref[...] + pair_product((lx_high[...], lx_low[...]), own_ref, other_ref)
    first = (row * rows_here + step * ROW_STEP) // block_len
    for s in range(sup_here):
        cols = slice(s * block_len, (s + 1) * block_len)
        chosen = []
        for part in range(ROW_STEP // block_len):
            kept = kept_columns(pattern_ref, widths_ref, first + part, sup + s)
            piece = total[cols, part * block_len : (part + 1) * block_len]
            chosen.append(jnp.where(subs < kept, -piece, 0.0))
        chosen = jnp.concatenate(chosen, axis=1)
        sel_ref[cols, :] = chosen
        crossed = dot3(split(chosen), (lm_high[:, cols], lm_low[:, cols]), ((1,), (0,)))

        @pl.when(step == 0)
        def _():
            cross_ref[cols, :] = crossed

        @pl.when(step != 0)
        def _():
            cross_ref[cols, :] += crossed


def per_device(mesh_sizes, inverse_panel, lower_blocks, diag_inverse, pattern, widths):
    row_count, col_count = mesh_sizes
    rows_here, _, _, run = inverse_panel.shape
    width = lower_blocks.shape[3]
    block_len = diag_inverse.shape[1]
    sup_here = width // block_len
    half = col_count // 2
    depth = row_count * rows_here
    col_index = lax.axis_index("pcol")

    row_bits = [1 << b for b in range(row_count.bit_length() - 1)]
    col_bits = [1 << b for b in range(1, col_count.bit_length() - 1)][::-1]
    row_orders = (row_bits, row_bits[::-1])

    def send(values, row_steps, col_step):
        pairs = []
        for r in range(row_count):
            for c in range(col_count):
                target = (r ^ row_steps[c % 2]) * col_count + (c ^ col_step)
                pairs.append((r * col_count + c, target))
        return lax.ppermute(values, ("prow", "pcol"), pairs)

    def along_rows(values, place):
        return send(values, [order[place] for order in row_orders], 0)

    def along_cols(values, place):
        return send(values, (0, 0), col_bits[place])

    def gathered(own, places, move):
        held = [own]
        for place in range(places):
            held = held + [move(values, place) for values in held]
        return held

    panel = jnp.transpose(inverse_panel, (1, 2, 3, 0)).reshape(row_count * run, rows_here)
    lower = lower_blocks.reshape(rows_here, width)
    lowers = gathered(lower, len(row_bits), along_rows)
    panels = gathered(panel, len(col_bits), along_cols)
    panels = [v for values in panels for v in (values, send(values, (0, 0), 1))]
    col_offsets = [offset_of(col_bits, block) for block in range(half)]

    shape = (row_count, col_count, run, block_len, sup_here)
    grid = (rows_here // ROW_STEP,)
    smem = pl.BlockSpec(memory_space=pltpu.SMEM)
    tall = row_count * run
    panel_spec = pl.BlockSpec((tall, ROW_STEP), lambda i: (0, i))
    total_spec = pl.BlockSpec((width, ROW_STEP), lambda i: (0, i))
    pair_spec = pl.BlockSpec((2 * tall, width), lambda i: (0, 0))
    early_bytes = 8 * depth * ROW_STEP + 8 * depth * width + 16 * rows_here * width
    total, *lower_parts = pl.pallas_call(
        functools.partial(early_kernel, shape, row_orders, col_offsets),
        grid=grid,
        in_specs=[panel_spec] * (2 * half - 2)
        + [pl.BlockSpec((rows_here, width), lambda i: (0, 0), pipeline_mode=pl.Buffered(1))]
        * row_count
        + [smem, smem],
        out_specs=[total_spec, pair_spec, pair_spec]
        + [pl.BlockSpec((rows_here, width), lambda i: (0, 0))] * 2,
        out_shape=[jax.ShapeDtypeStruct((width, rows_here), jnp.float32)]
        + [jax.ShapeDtypeStruct((2 * tall, width), jnp.bfloat16)] * 2
        + [jax.ShapeDtypeStruct((rows_here, width), jnp.bfloat16)] * 2,
        scratch_shapes=[pltpu.VMEM((depth, width), jnp.bfloat16)] * 2,
        compiler_params=pltpu.CompilerParams(vmem_limit_bytes=early_bytes + (6 << 20)),
        cost_estimate=pl.CostEstimate(
            flops=6 * depth * width * rows_here, bytes_accessed=8 << 20, transcendentals=0
        ),
    )(*panels[:-2], *lowers, pattern, widths)
    selected, crossed = pl.pallas_call(
        functools.partial(late_kernel, shape),
        grid=grid,
        in_specs=[total_spec, pair_spec, pair_spec]
        + [pl.BlockSpec((ROW_STEP, width), lambda i: (i, 0))] * 2
        + [panel_spec, panel_spec, smem, smem],
        out_specs=[total_spec, pl.BlockSpec((width, block_len), lambda i: (0, 0))],
        out_shape=[
            jax.ShapeDtypeStruct((width, rows_here), jnp.float32),
            jax.ShapeDtypeStruct((width, block_len), jnp.float32),
        ],
        compiler_params=pltpu.CompilerParams(vmem_limit_bytes=12 << 20),
    )(total, *lower_parts, *panels[-2:], pattern, widths)

    arrived = [send(crossed, (block, block), 0) for block in range(1, row_count)][::-1]
    for values in arrived:
        crossed = crossed + values
    widths_local = lax.dynamic_slice_in_dim(widths, col_index * sup_here, sup_here, 0)
    alive = jnp.arange(block_len, dtype=jnp.int32)[None, :] < widths_local[:, None]
    both_alive = alive[:, :, None] & alive[:, None, :]
    blocks = (sup_here, block_len, block_len)
    difference = diag_inverse.reshape(blocks) - crossed.reshape(blocks)
    diag_out = jnp.where(both_alive, difference, 0.0)
    return selected, diag_out.reshape(width, block_len)


def solution(mesh):
    placed = (
        P("prow", None, "pcol", None),
        P("prow", None, None, "pcol"),
        P("pcol", None),
        P(),
        P(),
    )
    return jax.shard_map(
        functools.partial(per_device, (mesh.shape["prow"], mesh.shape["pcol"])),
        mesh=mesh,
        in_specs=placed,
        out_specs=(P("pcol", "prow"), P("pcol", None)),
        check_vma=False,
    )
```

```python
import functools
import jax
import jax.numpy as jnp
from jax import lax
from jax.experimental import pallas as pl
from jax.experimental.pallas import tpu as pltpu
from jax.sharding import PartitionSpec as P

ROW_STEP = 256


def offset_of(order, block):
    total = 0
    for place, bit in enumerate(order):
        if block >> place & 1:
            total ^= bit
    return total


def split(values):
    high = values.astype(jnp.bfloat16)
    return high, (values - high.astype(jnp.float32)).astype(jnp.bfloat16)


def dot3(a, b, dims):
    (a_high, a_low), (b_high, b_low) = a, b
    dot = functools.partial(
        lax.dot_general, dimension_numbers=(dims, ((), ())), preferred_element_type=jnp.float32
    )
    return dot(a_high, b_high) + (dot(a_high, b_low) + dot(a_low, b_high))


def rows_of_pair(ref, source, run, rows_here, row_count):
    pieces = []
    for column in (source, source ^ 1):
        for i in range(row_count):
            base = pl.multiple_of(i * rows_here + column * run, run)
            pieces.append(ref[pl.ds(base, run), :])
    return jnp.concatenate(pieces, axis=0)


def pair_product(lowers, own, other):
    panel = [jnp.concatenate(halves, axis=0) for halves in zip(own, other)]
    return dot3(lowers, panel, ((0,), (0,)))


def own_kernel(shape, lower_ref, panel_ref, pattern_ref, widths_ref, *refs):
    _, col_count, run, block_len, sup_here = shape
    lm_high, lm_low, panel_high, panel_low, row_mask, sel_mask, diag_mask, *refs = refs
    lower, panel, lower_sem, panel_sem = refs
    rows_here = col_count * run
    step = pl.program_id(0)
    rows = pl.ds(pl.multiple_of(step * ROW_STEP, ROW_STEP), ROW_STEP)
    lower_copy = pltpu.make_async_copy(lower_ref.at[rows, :], lower, lower_sem)
    panel_copy = pltpu.make_async_copy(panel_ref.at[:, rows], panel, panel_sem)
    lower_copy.start()
    panel_copy.start()
    sup = lax.axis_index("pcol") * sup_here
    first = lax.axis_index("prow") * (rows_here // block_len) + step * (ROW_STEP // block_len)
    square = (block_len, block_len)
    lanes = lax.broadcasted_iota(jnp.int32, square, 1)
    subs = lax.broadcasted_iota(jnp.int32, square, 0)
    line = lax.broadcasted_iota(jnp.int32, (1, block_len), 1)

    def ones_where(kept):
        return jnp.where(kept, 1.0, 0.0).astype(jnp.float32)

    for s in range(sup_here):
        cols = slice(s * block_len, (s + 1) * block_len)
        width = widths_ref[sup + s]
        diag_mask[cols, :] = ones_where((lanes < width) & (subs < width))
        for row_block in range(row_mask.shape[0]):
            kept = jnp.where(pattern_ref[row_block, sup + s] != 0, width, 0)
            row_mask[row_block : row_block + 1, cols] = ones_where(line < kept)
        for part in range(ROW_STEP // block_len):
            here = slice(part * block_len, (part + 1) * block_len)
            kept = jnp.where(pattern_ref[first + part, sup + s] != 0, width, 0)
            sel_mask[cols, here] = ones_where(subs < kept)
    lower_copy.wait()
    for part in range(ROW_STEP // block_len):
        here = slice(part * block_len, (part + 1) * block_len)
        mask = row_mask[pl.ds(first + part, 1), :]
        lm_high[here, :], lm_low[here, :] = split(lower[here, :] * mask)
    panel_copy.wait()
    panel_high[...], panel_low[...] = split(panel[...])


def early_kernel(shape, row_orders, col_offsets, *refs):
    row_count, col_count, run, block_len, sup_here = shape
    half = col_count // 2
    own_panel, refs = refs[:2], refs[2:]
    panel_refs, refs = refs[: 2 * half - 3], refs[2 * half - 3 :]
    own_lower, refs = refs[:2], refs[2:]
    lower_refs, refs = refs[: row_count - 1], refs[row_count - 1 :]
    row_mask, total_ref, lx_high, lx_low, lh, ll = refs
    row = lax.axis_index("prow")
    col = lax.axis_index("pcol")
    core = lax.rem(col, 2)
    rows_here = col_count * run

    @pl.when(pl.program_id(0) == 0)
    def _():
        mine = pl.ds(pl.multiple_of(row * rows_here, rows_here), rows_here)
        lh[mine, :] = own_lower[0][...]
        ll[mine, :] = own_lower[1][...]
        for block, ref in enumerate(lower_refs):
            first, second = (offset_of(order, block + 1) for order in row_orders)
            source = row ^ jnp.where(core == 0, first, second)
            for part in range(rows_here // block_len):
                row_block = source * (rows_here // block_len) + part
                base = pl.multiple_of(row_block * block_len, block_len)
                here = slice(part * block_len, (part + 1) * block_len)
                high, low = split(ref[here, :] * row_mask[pl.ds(row_block, 1), :])
                lh[pl.ds(base, block_len), :] = high
                ll[pl.ds(base, block_len), :] = low
        late = col ^ col_offsets[-1]
        lx_high[...] = rows_of_pair(lh, late, run, rows_here, row_count)
        lx_low[...] = rows_of_pair(ll, late, run, rows_here, row_count)

    total = None
    for block in range(half - 1):
        source = col ^ col_offsets[block]
        lowers = tuple(rows_of_pair(ref, source, run, rows_here, row_count) for ref in (lh, ll))
        if block == 0:
            own = tuple(ref[...] for ref in own_panel)
        else:
            own = split(panel_refs[2 * block - 1][...])
        part = pair_product(lowers, own, split(panel_refs[2 * block][...]))
        total = part if total is None else total + part
    total_ref[...] = total


def late_kernel(shape, *refs):
    _, _, _, block_len, sup_here = shape
    total_ref, lx_high, lx_low, lm_high, lm_low, own_ref, other_ref, mask_ref, *refs = refs
    chosen_ref, cross_ref = refs
    step = pl.program_id(0)
    lowers = (lx_high[...], lx_low[...])
    total = total_ref[...] + pair_product(lowers, split(own_ref[...]), split(other_ref[...]))
    chosen_all = -total * mask_ref[...]
    chosen_ref[...] = chosen_all
    for s in range(sup_here):
        cols = slice(s * block_len, (s + 1) * block_len)
        chosen = split(chosen_all[cols, :])
        crossed = dot3(chosen, (lm_high[:, cols], lm_low[:, cols]), ((1,), (0,)))

        @pl.when(step == 0)
        def _():
            cross_ref[cols, :] = crossed

        @pl.when(step != 0)
        def _():
            cross_ref[cols, :] += crossed


def store_kernel(chosen_ref, out_ref):
    out_ref[...] = chosen_ref[...]


def per_device(mesh_sizes, inverse_panel, lower_blocks, diag_inverse, pattern, widths):
    row_count, col_count = mesh_sizes
    rows_here, _, _, run = inverse_panel.shape
    width = lower_blocks.shape[3]
    block_len = diag_inverse.shape[1]
    sup_here = width // block_len
    half = col_count // 2
    depth = row_count * rows_here
    tall = row_count * run

    row_bits = [1 << b for b in range(row_count.bit_length() - 1)]
    col_bits = [1 << b for b in range(1, col_count.bit_length() - 1)][::-1]
    row_orders = (row_bits, row_bits[::-1])
    col_offsets = [offset_of(col_bits, block) for block in range(half)]

    def send(values, row_steps, col_step):
        pairs = []
        for r in range(row_count):
            for c in range(col_count):
                target = (r ^ row_steps[c % 2]) * col_count + (c ^ col_step)
                pairs.append((r * col_count + c, target))
        return lax.ppermute(values, ("prow", "pcol"), pairs)

    def along_rows(values, place):
        return send(values, [order[place] for order in row_orders], 0)

    def along_cols(values, place):
        return send(values, (0, 0), col_bits[place])

    def to_other_core(values):
        return send(values, (0, 0), 1)

    def after(values, *others):
        return lax.optimization_barrier((values, *others))[0]

    panel = jnp.transpose(inverse_panel, (1, 2, 3, 0)).reshape(tall, rows_here)
    lower = lower_blocks.reshape(rows_here, width)

    shape = (row_count, col_count, run, block_len, sup_here)
    grid = (rows_here // ROW_STEP,)
    panel_spec = pl.BlockSpec((tall, ROW_STEP), lambda i: (0, i))
    total_spec = pl.BlockSpec((width, ROW_STEP), lambda i: (0, i))
    lower_spec = pl.BlockSpec((ROW_STEP, width), lambda i: (i, 0))

    def fixed(*dims):
        return pl.BlockSpec(dims, lambda i: (0, 0), pipeline_mode=pl.Buffered(1))

    def out_fixed(*dims):
        return pl.BlockSpec(dims, lambda i: (0, 0))

    def array(rows, columns, dtype=jnp.float32):
        return jax.ShapeDtypeStruct((rows, columns), dtype)

    small = pltpu.CompilerParams(vmem_limit_bytes=12 << 20)
    smem = pl.BlockSpec(memory_space=pltpu.SMEM)
    in_hbm = pl.BlockSpec(memory_space=pltpu.HBM)
    row_blocks = depth // block_len
    *own_lower, own_high, own_low, row_mask, sel_mask, diag_mask = pl.pallas_call(
        functools.partial(own_kernel, shape),
        grid=grid,
        in_specs=[in_hbm, in_hbm, smem, smem],
        out_specs=[lower_spec] * 2
        + [panel_spec] * 2
        + [out_fixed(row_blocks, width), total_spec, out_fixed(width, block_len)],
        out_shape=[array(rows_here, width, jnp.bfloat16)] * 2
        + [array(tall, rows_here, jnp.bfloat16)] * 2
        + [array(row_blocks, width), array(width, rows_here), array(width, block_len)],
        scratch_shapes=[
            pltpu.VMEM((ROW_STEP, width), jnp.float32),
            pltpu.VMEM((tall, ROW_STEP), jnp.float32),
            pltpu.SemaphoreType.DMA,
            pltpu.SemaphoreType.DMA,
        ],
        compiler_params=small,
    )(lower, panel, pattern, widths)

    lowers = [lower]
    for place in range(len(row_bits)):
        lowers = lowers + [along_rows(values, place) for values in lowers]
    panels = [panel]
    for place in range(len(col_bits)):
        panels = panels + [along_cols(values, place) for values in panels]
    pairs = [v for values in panels[:-1] for v in (values, to_other_core(values))]

    early_bytes = 8 * depth * ROW_STEP + 8 * depth * width + 12 * rows_here * width
    total, *lower_parts = pl.pallas_call(
        functools.partial(early_kernel, shape, row_orders, col_offsets),
        grid=grid,
        in_specs=[panel_spec] * (2 * half - 1)
        + [fixed(rows_here, width)] * (row_count + 1)
        + [fixed(row_blocks, width)],
        out_specs=[total_spec, out_fixed(2 * tall, width), out_fixed(2 * tall, width)],
        out_shape=[array(width, rows_here)] + [array(2 * tall, width, jnp.bfloat16)] * 2,
        scratch_shapes=[pltpu.VMEM((depth, width), jnp.bfloat16)] * 2,
        compiler_params=pltpu.CompilerParams(vmem_limit_bytes=early_bytes + (6 << 20)),
        cost_estimate=pl.CostEstimate(
            flops=6 * depth * width * rows_here, bytes_accessed=8 << 20, transcendentals=0
        ),
    )(own_high, own_low, *pairs[1:], *own_lower, *lowers[1:], row_mask)
    last = after(panels[-1], total)
    chosen, crossed = pl.pallas_call(
        functools.partial(late_kernel, shape),
        grid=grid,
        in_specs=[total_spec, fixed(2 * tall, width), fixed(2 * tall, width)]
        + [lower_spec] * 2
        + [panel_spec, panel_spec, total_spec],
        out_specs=[total_spec, out_fixed(width, block_len)],
        out_shape=[array(width, rows_here), array(width, block_len)],
        compiler_params=small,
    )(total, *lower_parts, *own_lower, last, to_other_core(last), sel_mask)
    selected = pl.pallas_call(
        store_kernel,
        grid=grid,
        in_specs=[total_spec],
        out_specs=total_spec,
        out_shape=array(width, rows_here),
        compiler_params=small,
    )(chosen)

    arrived = [send(crossed, (block, block), 0) for block in range(1, row_count)][::-1]
    for values in arrived:
        crossed = crossed + values
    return selected, (diag_inverse - crossed) * diag_mask


def solution(mesh):
    placed = (
        P("prow", None, "pcol", None),
        P("prow", None, None, "pcol"),
        P("pcol", None),
        P(),
        P(),
    )
    return jax.shard_map(
        functools.partial(per_device, (mesh.shape["prow"], mesh.shape["pcol"])),
        mesh=mesh,
        in_specs=placed,
        out_specs=(P("pcol", "prow"), P("pcol", None)),
        check_vma=False,
    )
```

```python
import functools
import jax
import jax.numpy as jnp
from jax import lax
from jax.experimental import pallas as pl
from jax.experimental.pallas import tpu as pltpu
from jax.sharding import PartitionSpec as P

ROW_STEP = 256


def offset_of(order, block):
    total = 0
    for place, bit in enumerate(order):
        if block >> place & 1:
            total ^= bit
    return total


def split(values):
    high = values.astype(jnp.bfloat16)
    return high, (values - high.astype(jnp.float32)).astype(jnp.bfloat16)


def dot3(a, b, dims):
    (a_high, a_low), (b_high, b_low) = a, b
    dot = functools.partial(
        lax.dot_general, dimension_numbers=(dims, ((), ())), preferred_element_type=jnp.float32
    )
    return dot(a_high, b_high) + (dot(a_high, b_low) + dot(a_low, b_high))


def rows_of_pair(ref, source, run, rows_here, row_count):
    pieces = []
    for column in (source, source ^ 1):
        for i in range(row_count):
            base = pl.multiple_of(i * rows_here + column * run, run)
            pieces.append(ref[pl.ds(base, run), :])
    return jnp.concatenate(pieces, axis=0)


def pair_product(lowers, own, other):
    panel = [jnp.concatenate(halves, axis=0) for halves in zip(own, other)]
    return dot3(lowers, panel, ((0,), (0,)))


def own_kernel(shape, lower_ref, panel_ref, pattern_ref, widths_ref, *refs):
    _, col_count, run, block_len, sup_here = shape
    lm_high, lm_low, panel_high, panel_low, row_mask, sel_mask, diag_mask, *refs = refs
    lower, panel, lower_sem, panel_sem = refs
    rows_here = col_count * run
    step = pl.program_id(0)
    rows = pl.ds(pl.multiple_of(step * ROW_STEP, ROW_STEP), ROW_STEP)
    lower_copy = pltpu.make_async_copy(lower_ref.at[rows, :], lower, lower_sem)
    panel_copy = pltpu.make_async_copy(panel_ref.at[:, rows], panel, panel_sem)
    lower_copy.start()
    panel_copy.start()
    sup = lax.axis_index("pcol") * sup_here
    first = lax.axis_index("prow") * (rows_here // block_len) + step * (ROW_STEP // block_len)
    square = (block_len, block_len)
    lanes = lax.broadcasted_iota(jnp.int32, square, 1)
    subs = lax.broadcasted_iota(jnp.int32, square, 0)
    line = lax.broadcasted_iota(jnp.int32, (1, block_len), 1)

    def ones_where(kept):
        return jnp.where(kept, 1.0, 0.0).astype(jnp.float32)

    for s in range(sup_here):
        cols = slice(s * block_len, (s + 1) * block_len)
        width = widths_ref[sup + s]
        diag_mask[cols, :] = ones_where((lanes < width) & (subs < width))
        for row_block in range(row_mask.shape[0]):
            kept = jnp.where(pattern_ref[row_block, sup + s] != 0, width, 0)
            row_mask[row_block : row_block + 1, cols] = ones_where(line < kept)
        for part in range(ROW_STEP // block_len):
            here = slice(part * block_len, (part + 1) * block_len)
            kept = jnp.where(pattern_ref[first + part, sup + s] != 0, width, 0)
            sel_mask[cols, here] = ones_where(subs < kept)
    lower_copy.wait()
    for part in range(ROW_STEP // block_len):
        here = slice(part * block_len, (part + 1) * block_len)
        mask = row_mask[pl.ds(first + part, 1), :]
        lm_high[here, :], lm_low[here, :] = split(lower[here, :] * mask)
    panel_copy.wait()
    panel_high[...], panel_low[...] = split(panel[...])


def early_kernel(shape, row_orders, col_offsets, *refs):
    row_count, col_count, run, block_len, sup_here = shape
    half = col_count // 2
    own_panel, refs = refs[:2], refs[2:]
    panel_refs, refs = refs[: 2 * half - 3], refs[2 * half - 3 :]
    own_lower, refs = refs[:2], refs[2:]
    lower_refs, refs = refs[: row_count - 1], refs[row_count - 1 :]
    row_mask, total_ref, lx_high, lx_low, lh, ll = refs
    row = lax.axis_index("prow")
    col = lax.axis_index("pcol")
    core = lax.rem(col, 2)
    rows_here = col_count * run

    @pl.when(pl.program_id(0) == 0)
    def _():
        mine = pl.ds(pl.multiple_of(row * rows_here, rows_here), rows_here)
        lh[mine, :] = own_lower[0][...]
        ll[mine, :] = own_lower[1][...]
        for block, ref in enumerate(lower_refs):
            first, second = (offset_of(order, block + 1) for order in row_orders)
            source = row ^ jnp.where(core == 0, first, second)
            for part in range(rows_here // block_len):
                row_block = source * (rows_here // block_len) + part
                base = pl.multiple_of(row_block * block_len, block_len)
                here = slice(part * block_len, (part + 1) * block_len)
                high, low = split(ref[here, :] * row_mask[pl.ds(row_block, 1), :])
                lh[pl.ds(base, block_len), :] = high
                ll[pl.ds(base, block_len), :] = low
        late = col ^ col_offsets[-1]
        lx_high[...] = rows_of_pair(lh, late, run, rows_here, row_count)
        lx_low[...] = rows_of_pair(ll, late, run, rows_here, row_count)

    total = None
    for block in range(half - 1):
        source = col ^ col_offsets[block]
        lowers = tuple(rows_of_pair(ref, source, run, rows_here, row_count) for ref in (lh, ll))
        if block == 0:
            own = tuple(ref[...] for ref in own_panel)
        else:
            own = split(panel_refs[2 * block - 1][...])
        part = pair_product(lowers, own, split(panel_refs[2 * block][...]))
        total = part if total is None else total + part
    total_ref[...] = total


def late_kernel(shape, *refs):
    _, _, _, block_len, sup_here = shape
    total_ref, lx_high, lx_low, lm_high, lm_low, own_ref, other_ref, mask_ref, *refs = refs
    chosen_ref, cross_ref = refs
    step = pl.program_id(0)
    lowers = (lx_high[...], lx_low[...])
    total = total_ref[...] + pair_product(lowers, split(own_ref[...]), split(other_ref[...]))
    chosen_all = -total * mask_ref[...]
    chosen_ref[...] = chosen_all
    for s in range(sup_here):
        cols = slice(s * block_len, (s + 1) * block_len)
        chosen = split(chosen_all[cols, :])
        crossed = dot3(chosen, (lm_high[:, cols], lm_low[:, cols]), ((1,), (0,)))

        @pl.when(step == 0)
        def _():
            cross_ref[cols, :] = crossed

        @pl.when(step != 0)
        def _():
            cross_ref[cols, :] += crossed


def store_kernel(chosen_ref, out_ref):
    out_ref[...] = chosen_ref[...]


def per_device(mesh_sizes, inverse_panel, lower_blocks, diag_inverse, pattern, widths):
    row_count, col_count = mesh_sizes
    rows_here, _, _, run = inverse_panel.shape
    width = lower_blocks.shape[3]
    block_len = diag_inverse.shape[1]
    sup_here = width // block_len
    half = col_count // 2
    depth = row_count * rows_here
    tall = row_count * run

    row_bits = [1 << b for b in range(row_count.bit_length() - 1)]
    col_bits = [1 << b for b in range(1, col_count.bit_length() - 1)][::-1]
    row_orders = (row_bits, row_bits[::-1])
    col_offsets = [offset_of(col_bits, block) for block in range(half)]

    def send(values, row_steps, col_step):
        pairs = []
        for r in range(row_count):
            for c in range(col_count):
                target = (r ^ row_steps[c % 2]) * col_count + (c ^ col_step)
                pairs.append((r * col_count + c, target))
        return lax.ppermute(values, ("prow", "pcol"), pairs)

    def along_rows(values, place):
        return send(values, [order[place] for order in row_orders], 0)

    def along_cols(values, place):
        return send(values, (0, 0), col_bits[place])

    def to_other_core(values):
        return send(values, (0, 0), 1)

    def after(values, *others):
        return lax.optimization_barrier((values, *others))[0]

    panel = jnp.transpose(inverse_panel, (1, 2, 3, 0)).reshape(tall, rows_here)
    lower = lower_blocks.reshape(rows_here, width)

    shape = (row_count, col_count, run, block_len, sup_here)
    grid = (rows_here // ROW_STEP,)
    panel_spec = pl.BlockSpec((tall, ROW_STEP), lambda i: (0, i))
    total_spec = pl.BlockSpec((width, ROW_STEP), lambda i: (0, i))
    lower_spec = pl.BlockSpec((ROW_STEP, width), lambda i: (i, 0))

    def fixed(*dims):
        return pl.BlockSpec(dims, lambda i: (0, 0), pipeline_mode=pl.Buffered(1))

    def out_fixed(*dims):
        return pl.BlockSpec(dims, lambda i: (0, 0))

    def array(rows, columns, dtype=jnp.float32):
        return jax.ShapeDtypeStruct((rows, columns), dtype)

    small = pltpu.CompilerParams(vmem_limit_bytes=12 << 20)
    smem = pl.BlockSpec(memory_space=pltpu.SMEM)
    in_hbm = pl.BlockSpec(memory_space=pltpu.HBM)
    row_blocks = depth // block_len
    *own_lower, own_high, own_low, row_mask, sel_mask, diag_mask = pl.pallas_call(
        functools.partial(own_kernel, shape),
        grid=grid,
        in_specs=[in_hbm, in_hbm, smem, smem],
        out_specs=[lower_spec] * 2
        + [panel_spec] * 2
        + [out_fixed(row_blocks, width), total_spec, out_fixed(width, block_len)],
        out_shape=[array(rows_here, width, jnp.bfloat16)] * 2
        + [array(tall, rows_here, jnp.bfloat16)] * 2
        + [array(row_blocks, width), array(width, rows_here), array(width, block_len)],
        scratch_shapes=[
            pltpu.VMEM((ROW_STEP, width), jnp.float32),
            pltpu.VMEM((tall, ROW_STEP), jnp.float32),
            pltpu.SemaphoreType.DMA,
            pltpu.SemaphoreType.DMA,
        ],
        compiler_params=small,
    )(*(pltpu.with_memory_space_constraint(v, pltpu.HBM) for v in (lower, panel, pattern, widths)))

    lowers = [lower]
    for place in range(len(row_bits)):
        lowers = lowers + [along_rows(values, place) for values in lowers]
    panels = [panel]
    for place in range(len(col_bits)):
        panels = panels + [along_cols(values, place) for values in panels]
    pairs = [panel, to_other_core(panel)]
    for values in panels[1:-1]:
        pairs += [values, to_other_core(after(values, own_high))]

    early_bytes = 8 * depth * ROW_STEP + 8 * depth * width + 12 * rows_here * width
    total, *lower_parts = pl.pallas_call(
        functools.partial(early_kernel, shape, row_orders, col_offsets),
        grid=grid,
        in_specs=[panel_spec] * (2 * half - 1)
        + [fixed(rows_here, width)] * (row_count + 1)
        + [fixed(row_blocks, width)],
        out_specs=[total_spec, out_fixed(2 * tall, width), out_fixed(2 * tall, width)],
        out_shape=[array(width, rows_here)] + [array(2 * tall, width, jnp.bfloat16)] * 2,
        scratch_shapes=[pltpu.VMEM((depth, width), jnp.bfloat16)] * 2,
        compiler_params=pltpu.CompilerParams(vmem_limit_bytes=early_bytes + (6 << 20)),
        cost_estimate=pl.CostEstimate(
            flops=6 * depth * width * rows_here, bytes_accessed=8 << 20, transcendentals=0
        ),
    )(own_high, own_low, *pairs[1:], *own_lower, *lowers[1:], row_mask)
    last = panels[-1]
    chosen, crossed = pl.pallas_call(
        functools.partial(late_kernel, shape),
        grid=grid,
        in_specs=[total_spec, fixed(2 * tall, width), fixed(2 * tall, width)]
        + [lower_spec] * 2
        + [panel_spec, panel_spec, total_spec],
        out_specs=[total_spec, out_fixed(width, block_len)],
        out_shape=[array(width, rows_here), array(width, block_len)],
        compiler_params=small,
    )(total, *lower_parts, *own_lower, last, to_other_core(last), sel_mask)
    selected = pl.pallas_call(
        store_kernel,
        grid=grid,
        in_specs=[total_spec],
        out_specs=total_spec,
        out_shape=array(width, rows_here),
        compiler_params=small,
    )(chosen)

    arrived = [send(crossed, (block, block), 0) for block in range(1, row_count)][::-1]
    for values in arrived:
        crossed = crossed + values
    return selected, (diag_inverse - crossed) * diag_mask


def solution(mesh):
    placed = (
        P("prow", None, "pcol", None),
        P("prow", None, None, "pcol"),
        P("pcol", None),
        P(),
        P(),
    )
    return jax.shard_map(
        functools.partial(per_device, (mesh.shape["prow"], mesh.shape["pcol"])),
        mesh=mesh,
        in_specs=placed,
        out_specs=(P("pcol", "prow"), P("pcol", None)),
        check_vma=False,
    )
```
